32 devices in a mesh: groups: 2 (over y), blk: 4 (over z), sub: 4 (over x, core).
Axes of the slice: x: 2, y: 2, z: 4, core: 2. Of those that a mesh axis runs over, the one named last changes fastest.
Arguments:
- train_grads: bfloat16 [20480, 2048], P(('groups', 'blk'), 'sub'), parts along dimension 0
- query_grads: bfloat16 [1024, 2048], P(('groups', 'blk'), 'sub'), parts along dimension 0
- train_ids: int32 [8, 2560], P(('groups', 'blk')), parts along dimension 0, may hold values from 0 to 2559, each once within a row
Outputs:
- scores: bfloat16 [8, 5, 2560, 128], P(('groups', 'blk'), None, 'sub'), parts along dimension 0
The draws below stay inside these ranges and needn't reach their ends.
There are 2 independent parts, one for each index of `groups`. The reference program is written for one: setup_inputs(seed, part) draws one part's arguments, and reference() takes and returns one part's arrays. A program takes and returns all parts, laid end to end along the dimension named above; each array names one. Nothing has to cross between parts.
Inputs may be any that keep to these rules, and one draw needn't show every extreme that they name: Each row of train_ids holds every id of one slab once.
All inputs are finite; a program needn't handle non-finite values.
Results may differ from the reference program's by a relative error of at most 0.01.
Values may be sent and summed in bfloat16 or wider, within the bound.
A program may use at most 64 MiB of HBM per device.

```python
import math
import jax
import jax.numpy as jnp
from jax import lax

K = 2048
TR = 2560
QB = 128
HOPS = 2
NTRAIN = 10240
NQ = 512
N_BLK = 4
N_SUB = 4


def column_scales(key):
    rising = 3.0 ** (jnp.arange(K, dtype=jnp.float32) / K)
    rough = jnp.exp(jax.random.uniform(key, (K,), jnp.float32, 0.0, math.log(3.4)))
    return rising * rough


def gradient_rows(key, count):
    keys = jax.random.split(key, 3)
    row_scale = jnp.exp(jax.random.uniform(keys[0], (count, 1), jnp.float32, 0.0, math.log(10.0)))
    cols = column_scales(keys[1])
    base = jax.random.normal(keys[2], (count, K), jnp.float32)
    return base * row_scale * cols * 0.1


def draw_train_grads(key, part):
    key = jax.random.fold_in(key, 11)
    return gradient_rows(key, NTRAIN).astype(jnp.bfloat16)


def draw_query_grads(key, part):
    key = jax.random.fold_in(key, 12)
    return gradient_rows(key, NQ).astype(jnp.bfloat16)


def setup_inputs(seed: int = 0, part: int = 0) -> dict:
    arg_keys = jax.random.split(jax.random.key(seed), 4)
    own_keys = jax.random.split(jax.random.fold_in(arg_keys[3], part), 4)
    return {
        "train_grads": draw_train_grads(jax.random.fold_in(jax.random.fold_in(arg_keys[3], part), 71), part),
        "query_grads": draw_query_grads(jax.random.fold_in(jax.random.fold_in(arg_keys[3], part), 71), part),
        "train_ids": jax.vmap(lambda own: jax.random.permutation(own, TR))(jax.random.split(own_keys[2], N_BLK)).reshape((N_BLK, TR)).astype(jnp.int32),
    }


EPS = 1e-06

def reference(train_grads, query_grads, train_ids):
    win = 2 * HOPS + 1
    width = K // N_SUB
    slabs = train_grads.reshape(N_BLK, TR, K)
    inverse = jnp.argsort(train_ids, axis=1, stable=True).astype(jnp.int32)
    ordered = jnp.take_along_axis(slabs, inverse[:, :, None], axis=1)
    train_sq = lax.optimization_barrier(jnp.sum(jnp.square(ordered.astype(jnp.float32)), axis=2))
    train_scale = (lax.rsqrt(train_sq / K + EPS) * K ** (-0.5)).astype(jnp.bfloat16)
    blocks = query_grads.reshape(N_BLK, QB, K)
    query_sq = lax.optimization_barrier(jnp.sum(jnp.square(blocks.astype(jnp.float32)), axis=2))
    query_scale = lax.rsqrt(query_sq / K + EPS)
    offsets = jnp.arange(-HOPS, HOPS + 1, dtype=jnp.int32)

    def one_slab(slab):
        index = (slab + offsets) % N_BLK
        window = blocks[index].astype(jnp.float32).reshape(win, QB, N_SUB, width)
        rows = ordered[slab].astype(jnp.float32).reshape(TR, N_SUB, width)
        part = jnp.einsum('tpk,wjpk->pwtj', rows, window, precision=lax.Precision.HIGHEST)
        part = part.astype(jnp.bfloat16).astype(jnp.float32)
        raw = lax.optimization_barrier(jnp.sum(part, axis=0))
        return (raw * train_scale[slab].astype(jnp.float32)[None, :, None]).astype(jnp.bfloat16)
    tiles = lax.map(one_slab, jnp.arange(N_BLK, dtype=jnp.int32))
    block_idx = jnp.arange(N_BLK, dtype=jnp.int32)[:, None]
    slot_idx = jnp.arange(win, dtype=jnp.int32)[None, :]
    source = (block_idx - slot_idx + HOPS) % N_BLK
    placed = tiles[source, slot_idx]
    return (placed.astype(jnp.float32) * query_scale[:, None, None, :]).astype(jnp.bfloat16)
```

```python
import functools
import math

import jax
import jax.numpy as jnp
from jax import lax
from jax.experimental import pallas as pl
from jax.experimental.pallas import tpu as pltpu
from jax.sharding import PartitionSpec as P

HOPS = 2
EPS = 1e-06
LANES = 128
MESH = pl.DeviceIdType.MESH
F32 = jnp.float32
BF16 = jnp.bfloat16


def distinct_offsets(n_blk):
    found = []
    for d in sorted(range(-HOPS, HOPS + 1), key=lambda d: (abs(d), d)):
        if d % n_blk not in found:
            found.append(d % n_blk)
    return found


def kernel(
    n_blk, n_sub, train, query, ids, out,
    ordered, qwin, pown, snd1, rcv1, snd2, rcv2, snd3, rcv3, stat_s, stat_r, scale,
    q_ss, q_rs, s1_ss, s1_rs, s2_ss, s2_rs, s3_ss, s3_rs, st_ss, st_rs,
):
    offsets = distinct_offsets(n_blk)
    nd = len(offsets)
    nx = n_sub // 2
    rows, width = train.shape
    block_rows = query.shape[0]
    share = rows // n_sub
    full = width * n_sub
    lanes = math.gcd(share, LANES)
    blocks = share // lanes
    chunk = share
    while chunk > 320 and chunk % 32 == 0:
        chunk //= 2

    g, z, p = lax.axis_index("groups"), lax.axis_index("blk"), lax.axis_index("sub")
    x, k = p // 2, p % 2

    def sub_peer(kk, j):
        return (g, z, 2 * ((x + j) % nx) + (k if kk else 1 - k))

    def blk_peer(e):
        return (g, (z + e) % n_blk, p)

    order = [j % nx for j in range(1, nx + 1)]

    barrier = pltpu.get_barrier_semaphore()
    peers = [sub_peer(kk, j) for kk in (0, 1) for j in range(nx) if (kk, j) != (1, 0)]
    peers += [blk_peer(e) for e in offsets if e]
    for peer in peers:
        pl.semaphore_signal(barrier, inc=1, device_id=peer, device_id_type=MESH)

    def remote(src, dst, send, recv, peer):
        return pltpu.make_async_remote_copy(
            src_ref=src, dst_ref=dst, send_sem=send, recv_sem=recv,
            device_id=peer, device_id_type=MESH,
        )

    started = []

    def start(copy):
        copy.start()
        started.append(copy)
        return copy

    eye = (
        lax.broadcasted_iota(jnp.int32, (lanes, LANES), 0)
        == lax.broadcasted_iota(jnp.int32, (lanes, LANES), 1)
    )
    eye_q = (
        lax.broadcasted_iota(jnp.int32, (block_rows, LANES), 0)
        == lax.broadcasted_iota(jnp.int32, (block_rows, LANES), 1)
    )

    def to_row(column, mask):
        return jnp.sum(jnp.where(mask, column, 0.0), axis=0, keepdims=True)

    qf = query[...].astype(F32)
    query_row = to_row(jnp.sum(qf * qf, axis=1, keepdims=True), eye_q)

    pl.semaphore_wait(barrier, len(peers))

    query_copies = {}
    for i, e in enumerate(offsets):
        if e:
            query_copies[i] = start(
                remote(query, qwin.at[i], q_ss.at[i], q_rs.at[i], blk_peer(n_blk - e))
            )

    def window(i):
        return query if i == 0 else qwin.at[i]

    copies1, copies2, copies3, stat_copies = {}, {}, {}, {}

    def product(i, kk, j, at):
        value = lax.dot_general(
            ordered[kk, j, at, :], window(i)[...], (((1,), (1,)), ((), ())),
            preferred_element_type=F32,
        )
        if kk:
            pown[i, j, at, :] = value
        else:
            snd1[i, j, at, :] = value.astype(BF16)

    def send1(i, j):
        copies1[i, j] = start(
            remote(
                snd1.at[i, j], rcv1.at[i, j], s1_ss.at[i, j], s1_rs.at[i, j], sub_peer(0, 0)
            )
        )

    def permute(kk, j):
        slot = kk * nx + j
        q = 2 * ((x + j) % nx) + (k if kk else 1 - k)

        def step(c, carry):
            first = pl.multiple_of(c * chunk, chunk)
            at = pl.ds(first, chunk)
            wanted = lax.broadcasted_iota(jnp.int32, (chunk, rows), 0) + (q * share + first)
            hot = jnp.where(wanted == ids[...], 1.0, 0.0).astype(BF16)
            value = jnp.dot(hot, train[...], preferred_element_type=F32)
            ordered[kk, j, at, :] = value.astype(BF16)
            scale[at, :] = jnp.broadcast_to(
                jnp.sum(value * value, axis=1, keepdims=True), (chunk, LANES)
            )
            product(0, kk, j, at)
            return carry

        lax.fori_loop(0, share // chunk, step, 0)
        for b in range(blocks):
            stat_s[slot, b : b + 1, :] = to_row(scale[b * lanes : (b + 1) * lanes, :], eye)
        stat_s[slot, blocks : blocks + 1, :] = query_row
        if kk == 0:
            send1(0, j)
        if slot != nx:
            stat_copies[slot] = start(
                remote(
                    stat_s.at[slot], stat_r.at[slot], st_ss.at[slot], st_rs.at[slot],
                    sub_peer(kk, j),
                )
            )

    def stage_a(i):
        query_copies[i].wait_recv()
        for j in order:
            for kk in (0, 1):

                def step(c, carry):
                    product(i, kk, j, pl.ds(pl.multiple_of(c * chunk, chunk), chunk))
                    return carry

                lax.fori_loop(0, share // chunk, step, 0)
                if kk == 0:
                    send1(i, j)

    def stage_b(i, j):
        copies1[i, j].wait_recv()
        total = pown[i, j] + rcv1[i, j].astype(F32)
        if j:
            snd2[i, j] = total.astype(BF16)
            copies2[i, j] = start(
                remote(
                    snd2.at[i, j], rcv2.at[i, j], s2_ss.at[i, j], s2_rs.at[i, j], sub_peer(1, j)
                )
            )
        else:
            pown[i, 0] = total

    def stage_c(i):
        total = pown[i, 0]
        for j in range(1, nx):
            copies2[i, j].wait_recv()
            total += rcv2[i, j].astype(F32)
        snd3[i] = (total * scale[...]).astype(BF16)
        if offsets[i]:
            copies3[i] = start(
                remote(snd3.at[i], rcv3.at[i], s3_ss.at[i], s3_rs.at[i], blk_peer(offsets[i]))
            )

    for j in order:
        for kk in (0, 1):
            permute(kk, j)
        stage_b(0, j)

    stats = stat_s[nx]
    for slot in range(n_sub):
        if slot != nx:
            stat_copies[slot].wait_recv()
            stats += stat_r[slot]
    train_rows = (lax.rsqrt(stats / full + EPS) * full ** (-0.5)).astype(BF16).astype(F32)
    query_scale = lax.rsqrt(stats[blocks : blocks + 1, :] / full + EPS)
    for b in range(blocks):
        column = jnp.sum(
            jnp.where(eye, train_rows[b : b + 1, :], 0.0), axis=1, keepdims=True
        )
        scale[b * lanes : (b + 1) * lanes, :] = jnp.broadcast_to(column, (lanes, LANES))

    def finish(i):
        tile = (rcv3 if offsets[i] else snd3)[i].astype(F32)
        scored = (tile * query_scale).astype(BF16)
        for w in range(2 * HOPS + 1):
            if (w - HOPS) % n_blk == offsets[i]:
                out[0, w] = scored

    for t in range(1, nd + 2):
        if t < nd:
            stage_a(t)
        if 1 <= t - 1 < nd:
            for j in order:
                stage_b(t - 1, j)
        if 0 <= t - 2 < nd:
            stage_c(t - 2)
    for i in range(nd):
        if i:
            copies3[i].wait_recv()
        finish(i)
    for copy in started:
        copy.wait_send()


def local(n_blk, n_sub, train_grads, query_grads, train_ids):
    rows, width = train_grads.shape
    block_rows = query_grads.shape[0]
    share = rows // n_sub
    nx = n_sub // 2
    nd = len(distinct_offsets(n_blk))
    stat_rows = -(-(share // math.gcd(share, LANES) + 1) // 8) * 8
    win = 2 * HOPS + 1
    dma = pltpu.SemaphoreType.DMA
    vmem = pl.BlockSpec(memory_space=pltpu.VMEM)
    return pl.pallas_call(
        functools.partial(kernel, n_blk, n_sub),
        out_shape=jax.ShapeDtypeStruct((1, win, share, block_rows), BF16),
        in_specs=[vmem] * 3,
        out_specs=vmem,
        scratch_shapes=[
            pltpu.VMEM((2, nx, share, width), BF16),
            pltpu.VMEM((nd, block_rows, width), BF16),
            pltpu.VMEM((nd, nx, share, block_rows), F32),
            pltpu.VMEM((nd, nx, share, block_rows), BF16),
            pltpu.VMEM((nd, nx, share, block_rows), BF16),
            pltpu.VMEM((nd, nx, share, block_rows), BF16),
            pltpu.VMEM((nd, nx, share, block_rows), BF16),
            pltpu.VMEM((nd, share, block_rows), BF16),
            pltpu.VMEM((nd, share, block_rows), BF16),
            pltpu.VMEM((n_sub, stat_rows, LANES), F32),
            pltpu.VMEM((n_sub, stat_rows, LANES), F32),
            pltpu.VMEM((share, LANES), F32),
            dma((nd,)), dma((nd,)),
            dma((nd, nx)), dma((nd, nx)),
            dma((nd, nx)), dma((nd, nx)),
            dma((nd,)), dma((nd,)),
            dma((n_sub,)), dma((n_sub,)),
        ],
        compiler_params=pltpu.CompilerParams(
            collective_id=0, has_side_effects=True, vmem_limit_bytes=48 * 1024 * 1024
        ),
    )(train_grads, query_grads, train_ids)


def solution(mesh):
    return jax.shard_map(
        functools.partial(local, mesh.shape["blk"], mesh.shape["sub"]),
        mesh=mesh,
        in_specs=(
            P(("groups", "blk"), "sub"),
            P(("groups", "blk"), "sub"),
            P(("groups", "blk"), None),
        ),
        out_specs=P(("groups", "blk"), None, "sub", None),
        check_vma=False,
    )
```

```python
import functools
import math

import jax
import jax.numpy as jnp
from jax import lax
from jax.experimental import pallas as pl
from jax.experimental.pallas import tpu as pltpu
from jax.sharding import PartitionSpec as P

HOPS = 2
EPS = 1e-06
LANES = 128
PARTS = 2
MESH = pl.DeviceIdType.MESH
F32 = jnp.float32
BF16 = jnp.bfloat16


def distinct_offsets(n_blk):
    if n_blk == 4:
        return [0, 1, 2, 3]
    found = []
    for d in sorted(range(-HOPS, HOPS + 1), key=lambda d: (abs(d), d)):
        if d % n_blk not in found:
            found.append(d % n_blk)
    return found


def pick(cond, a, b):
    return lax.select(cond, jnp.int32(a), jnp.int32(b))


def kernel(
    n_blk, n_sub, train_in, query_in, ids_in, out,
    train, query, ids, ordered, qwin, pown, snd1, rcv1, snd2, rcv2, snd3, rcv3,
    stat_s, stat_r, squares, scale,
    in_s, q_ss, q_rs, s1_ss, s1_rs, s2_ss, s2_rs, s3_ss, s3_rs, st_ss, st_rs,
):
    offsets = distinct_offsets(n_blk)
    line = n_blk == 4
    nd = len(offsets)
    nx = n_sub // 2
    rows, width = train.shape
    block_rows = query.shape[0]
    share = rows // n_sub
    half = share // PARTS
    full = width * n_sub
    lanes = math.gcd(half, LANES)
    blocks = half // lanes

    loads = [
        pltpu.make_async_copy(src, dst, in_s.at[n])
        for n, (src, dst) in enumerate(((query_in, query), (ids_in, ids), (train_in, train)))
    ]
    for load in loads:
        load.start()

    g, z, p = lax.axis_index("groups"), lax.axis_index("blk"), lax.axis_index("sub")
    x, k = p // 2, p % 2

    def sub_peer(kk, j):
        return (g, z, 2 * ((x + j) % nx) + (k if kk else 1 - k))

    def blk_peer(e):
        return (g, (z + e) % n_blk, p)

    order = [j % nx for j in range(1, nx + 1)]

    barrier = pltpu.get_barrier_semaphore()
    peers = [sub_peer(kk, j) for kk in (0, 1) for j in range(nx) if (kk, j) != (1, 0)]
    peers += [blk_peer(e) for e in offsets if e]
    for peer in peers:
        pl.semaphore_signal(barrier, inc=1, device_id=peer, device_id_type=MESH)

    def remote(src, dst, send, recv, peer):
        return pltpu.make_async_remote_copy(
            src_ref=src, dst_ref=dst, send_sem=send, recv_sem=recv,
            device_id=peer, device_id_type=MESH,
        )

    started = []

    def start(copy):
        copy.start()
        started.append(copy)
        return copy

    eye = (
        lax.broadcasted_iota(jnp.int32, (lanes, LANES), 0)
        == lax.broadcasted_iota(jnp.int32, (lanes, LANES), 1)
    )
    eye_q = (
        lax.broadcasted_iota(jnp.int32, (block_rows, LANES), 0)
        == lax.broadcasted_iota(jnp.int32, (block_rows, LANES), 1)
    )

    def to_row(column, mask):
        return jnp.sum(jnp.where(mask, column, 0.0), axis=0, keepdims=True)

    loads[0].wait()
    qf = query[...].astype(F32)
    query_row = to_row(jnp.sum(qf * qf, axis=1, keepdims=True), eye_q)

    if line:
        even = z % 2 == 0
        mirror = pick(even, 3, 1)
        partner = 4 - mirror

        def send_query(src, dst, n, to):
            return remote(query if src is None else qwin.at[src], qwin.at[dst],
                          q_ss.at[n], q_rs.at[dst], blk_peer(to))

        handed = send_query(mirror, 2, 2, partner)

        def position(t):
            return (0, mirror, partner, 2)[t]

    else:

        def position(t):
            return t

    def send_queries():
        if line:
            start(send_query(None, partner, 0, mirror))
            start(send_query(None, mirror, 1, partner))
        else:
            for i, e in enumerate(offsets):
                if e:
                    start(remote(query, qwin.at[i], q_ss.at[i], q_rs.at[i], blk_peer(n_blk - e)))

    def wait_query(t):
        i = position(t)
        remote(query, qwin.at[i], q_ss.at[0], q_rs.at[i], blk_peer(1)).wait_recv()
        if line and t == 1:
            start(handed)

    def offset_at(t):
        return position(t) if line else offsets[t]

    copies1, copies2, copies3, stat_copies = {}, {}, {}, {}

    def part(h):
        return pl.ds(h * half, half)

    def product(t, kk, j, h):
        window = query[...] if t == 0 else qwin[position(t)]
        value = lax.dot_general(
            ordered[kk, j, part(h), :], window, (((1,), (1,)), ((), ())),
            preferred_element_type=F32,
        )
        if kk:
            pown[t, j, part(h), :] = value
        else:
            snd1[t, j, part(h), :] = value.astype(BF16)
            copies1[t, j, h] = start(
                remote(
                    snd1.at[t, j, part(h)], rcv1.at[t, j, part(h)],
                    s1_ss.at[t, j, h], s1_rs.at[t, j, h], sub_peer(0, 0),
                )
            )

    def permute(kk, j, h):
        slot = kk * nx + j
        q = 2 * ((x + j) % nx) + (k if kk else 1 - k)
        wanted = lax.broadcasted_iota(jnp.int32, (half, rows), 0) + (q * share + h * half)
        hot = jnp.where(wanted == ids[...], 1.0, 0.0).astype(BF16)
        value = jnp.dot(hot, train[...], preferred_element_type=F32)
        ordered[kk, j, part(h), :] = value.astype(BF16)
        squares[...] = jnp.broadcast_to(
            jnp.sum(value * value, axis=1, keepdims=True), (half, LANES)
        )
        for b in range(blocks):
            stat_s[slot, h, b : b + 1, :] = to_row(squares[b * lanes : (b + 1) * lanes, :], eye)
        stat_s[slot, h, blocks : blocks + 1, :] = query_row

    def send_stats(h):
        for kk in (0, 1):
            for j in range(nx):
                slot = kk * nx + j
                if slot != nx:
                    stat_copies[slot, h] = start(
                        remote(
                            stat_s.at[slot, h], stat_r.at[slot, h],
                            st_ss.at[slot, h], st_rs.at[slot, h], sub_peer(kk, j),
                        )
                    )

    def stage_a(t, h):
        for j in order:
            for kk in (0, 1):
                product(t, kk, j, h)

    def stage_b(t, h):
        for j in order:
            copies1[t, j, h].wait_recv()
            total = pown[t, j, part(h), :] + rcv1[t, j, part(h), :].astype(F32)
            if j:
                snd2[t, j, part(h), :] = total.astype(BF16)
                copies2[t, j, h] = start(
                    remote(
                        snd2.at[t, j, part(h)], rcv2.at[t, j, part(h)],
                        s2_ss.at[t, j, h], s2_rs.at[t, j, h], sub_peer(1, j),
                    )
                )
            else:
                pown[t, 0, part(h), :] = total

    query_scale = []

    def scales(h):
        stats = stat_s[nx, h]
        for slot in range(n_sub):
            if slot != nx:
                stat_copies[slot, h].wait_recv()
                stats += stat_r[slot, h]
        values = (lax.rsqrt(stats / full + EPS) * full ** (-0.5)).astype(BF16).astype(F32)
        query_scale.append(lax.rsqrt(stats[blocks : blocks + 1, :] / full + EPS))
        for b in range(blocks):
            column = jnp.sum(
                jnp.where(eye, values[b : b + 1, :], 0.0), axis=1, keepdims=True
            )
            scale[pl.ds(h * half + b * lanes, lanes), :] = jnp.broadcast_to(
                column, (lanes, LANES)
            )

    def stage_c(t, h):
        total = pown[t, 0, part(h), :]
        for j in range(1, nx):
            copies2[t, j, h].wait_recv()
            total += rcv2[t, j, part(h), :].astype(F32)
        tile = (total * scale[part(h), :]).astype(BF16)
        if t:
            i = position(t)
            snd3[t, part(h), :] = tile
            copies3[t, h] = start(
                remote(
                    snd3.at[t, part(h)], rcv3.at[i, part(h)],
                    s3_ss.at[t, h], s3_rs.at[i, h], blk_peer(offset_at(t)),
                )
            )
        else:
            write(0, h, tile)

    def write(i, h, tile):
        scored = (tile.astype(F32) * query_scale[0]).astype(BF16)
        for w in range(2 * HOPS + 1):
            if (w - HOPS) % n_blk == offsets[i]:
                out[0, w, part(h), :] = scored

    loads[1].wait()
    loads[2].wait()
    def arrange(h, js):
        for j in js:
            for kk in (0, 1):
                permute(kk, j, h)

    arrange(0, order)
    pl.semaphore_wait(barrier, len(peers))
    send_queries()
    stage_a(0, 0)
    send_stats(0)
    arrange(1, order[: nx // 2])
    stage_b(0, 0)
    arrange(1, order[nx // 2 :])
    stage_a(0, 1)
    send_stats(1)
    stage_b(0, 1)
    wait_query(1)
    stage_a(1, 0)
    stage_a(1, 1)
    scales(0)
    stage_b(1, 0)
    stage_b(1, 1)
    scales(1)
    wait_query(2)
    for h in range(PARTS):
        stage_a(2, h)
    for h in range(PARTS):
        stage_b(2, h)
    for h in range(PARTS):
        stage_c(1, h)
    for t in range(3, nd):
        wait_query(t)
        for h in range(PARTS):
            stage_a(t, h)
        for h in range(PARTS):
            stage_b(t, h)
        for h in range(PARTS):
            stage_c(t - 1, h)
    for t in (0, nd - 1):
        for h in range(PARTS):
            stage_c(t, h)

    for h in range(PARTS):
        for i in range(1, nd):
            remote(
                snd3.at[i, part(h)], rcv3.at[i, part(h)],
                s3_ss.at[i, h], s3_rs.at[i, h], blk_peer(1),
            ).wait_recv()
            write(i, h, rcv3[i, part(h), :])
    for copy in started:
        copy.wait_send()


def local(n_blk, n_sub, train_grads, query_grads, train_ids):
    rows, width = train_grads.shape
    block_rows = query_grads.shape[0]
    share = rows // n_sub
    half = share // PARTS
    nx = n_sub // 2
    nd = len(distinct_offsets(n_blk))
    stat_rows = -(-(half // math.gcd(half, LANES) + 1) // 8) * 8
    win = 2 * HOPS + 1
    dma = pltpu.SemaphoreType.DMA
    hbm = pl.BlockSpec(memory_space=pl.ANY)
    sums = (nd, nx, share, block_rows)
    return pl.pallas_call(
        functools.partial(kernel, n_blk, n_sub),
        out_shape=jax.ShapeDtypeStruct((1, win, share, block_rows), BF16),
        in_specs=[hbm] * 3,
        out_specs=pl.BlockSpec(memory_space=pltpu.VMEM),
        scratch_shapes=[
            pltpu.VMEM((rows, width), BF16),
            pltpu.VMEM((block_rows, width), BF16),
            pltpu.VMEM((1, rows), jnp.int32),
            pltpu.VMEM((2, nx, share, width), BF16),
            pltpu.VMEM((nd, block_rows, width), BF16),
            pltpu.VMEM(sums, F32),
            pltpu.VMEM(sums, BF16),
            pltpu.VMEM(sums, BF16),
            pltpu.VMEM(sums, BF16),
            pltpu.VMEM(sums, BF16),
            pltpu.VMEM((nd, share, block_rows), BF16),
            pltpu.VMEM((nd, share, block_rows), BF16),
            pltpu.VMEM((n_sub, PARTS, stat_rows, LANES), F32),
            pltpu.VMEM((n_sub, PARTS, stat_rows, LANES), F32),
            pltpu.VMEM((half, LANES), F32),
            pltpu.VMEM((share, LANES), F32),
            dma((3,)), dma((max(nd, 4),)), dma((nd,)),
            dma((nd, nx, PARTS)), dma((nd, nx, PARTS)),
            dma((nd, nx, PARTS)), dma((nd, nx, PARTS)),
            dma((nd, PARTS)), dma((nd, PARTS)),
            dma((n_sub, PARTS)), dma((n_sub, PARTS)),
        ],
        compiler_params=pltpu.CompilerParams(
            collective_id=0, has_side_effects=True, vmem_limit_bytes=56 * 1024 * 1024
        ),
    )(train_grads, query_grads, train_ids)


def solution(mesh):
    return jax.shard_map(
        functools.partial(local, mesh.shape["blk"], mesh.shape["sub"]),
        mesh=mesh,
        in_specs=(
            P(("groups", "blk"), "sub"),
            P(("groups", "blk"), "sub"),
            P(("groups", "blk"), None),
        ),
        out_specs=P(("groups", "blk"), None, "sub", None),
        check_vma=False,
    )
```

```python
import functools
import math

import jax
import jax.numpy as jnp
from jax import lax
from jax.experimental import pallas as pl
from jax.experimental.pallas import tpu as pltpu
from jax.sharding import PartitionSpec as P

HOPS = 2
EPS = 1e-06
LANES = 128
PARTS = 2
MESH = pl.DeviceIdType.MESH
F32 = jnp.float32
BF16 = jnp.bfloat16


def distinct_offsets(n_blk):
    if n_blk == 4:
        return [0, 1, 2, 3]
    found = []
    for d in sorted(range(-HOPS, HOPS + 1), key=lambda d: (abs(d), d)):
        if d % n_blk not in found:
            found.append(d % n_blk)
    return found


def pick(cond, a, b):
    return lax.select(cond, jnp.int32(a), jnp.int32(b))


def kernel(
    n_blk, n_sub, train_in, query_in, ids_in, out,
    train, query, ids, ordered, qwin, pown, snd1, rcv1, snd2, rcv2, snd3, rcv3,
    stat_s, stat_r, squares, scale,
    in_s, q_ss, q_rs, s1_ss, s1_rs, s2_ss, s2_rs, s3_ss, s3_rs, st_ss, st_rs,
):
    offsets = distinct_offsets(n_blk)
    line = n_blk == 4
    nd = len(offsets)
    nx = n_sub // 2
    rows, width = train.shape
    block_rows = query.shape[0]
    share = rows // n_sub
    half = share // PARTS
    full = width * n_sub
    lanes = math.gcd(half, LANES)
    blocks = half // lanes

    loads = [
        pltpu.make_async_copy(src, dst, in_s.at[n])
        for n, (src, dst) in enumerate(((query_in, query), (ids_in, ids), (train_in, train)))
    ]
    for load in loads:
        load.start()

    g, z, p = lax.axis_index("groups"), lax.axis_index("blk"), lax.axis_index("sub")
    x, k = p // 2, p % 2

    def sub_peer(kk, j):
        return (g, z, 2 * ((x + j) % nx) + (k if kk else 1 - k))

    def blk_peer(e):
        return (g, (z + e) % n_blk, p)

    order = [j % nx for j in range(1, nx + 1)]

    barrier = pltpu.get_barrier_semaphore()
    peers = [sub_peer(kk, j) for kk in (0, 1) for j in range(nx) if (kk, j) != (1, 0)]
    peers += [blk_peer(e) for e in offsets if e]
    for peer in peers:
        pl.semaphore_signal(barrier, inc=1, device_id=peer, device_id_type=MESH)

    def remote(src, dst, send, recv, peer):
        return pltpu.make_async_remote_copy(
            src_ref=src, dst_ref=dst, send_sem=send, recv_sem=recv,
            device_id=peer, device_id_type=MESH,
        )

    started = []

    def start(copy):
        copy.start()
        started.append(copy)
        return copy

    eye = (
        lax.broadcasted_iota(jnp.int32, (lanes, LANES), 0)
        == lax.broadcasted_iota(jnp.int32, (lanes, LANES), 1)
    )
    eye_q = (
        lax.broadcasted_iota(jnp.int32, (block_rows, LANES), 0)
        == lax.broadcasted_iota(jnp.int32, (block_rows, LANES), 1)
    )

    def to_row(column, mask):
        return jnp.sum(jnp.where(mask, column, 0.0), axis=0, keepdims=True)

    loads[0].wait()
    qf = query[...].astype(F32)
    query_row = to_row(jnp.sum(qf * qf, axis=1, keepdims=True), eye_q)

    if line:
        even = z % 2 == 0
        mirror = pick(even, 3, 1)
        partner = 4 - mirror

        def send_query(src, dst, n, to):
            return remote(query if src is None else qwin.at[src], qwin.at[dst],
                          q_ss.at[n], q_rs.at[dst], blk_peer(to))

        inner = (z == 1) | (z == 2)
        to_mirror = send_query(None, partner, 0, mirror)
        to_partner = send_query(None, mirror, 1, partner)
        handed = send_query(mirror, 2, 2, partner)

        def position(t):
            return (0, mirror, partner, 2)[t]

    else:

        def position(t):
            return t

    def send_queries():
        if line:
            start(to_partner)

            @pl.when(inner)
            def _():
                to_mirror.start()

        else:
            for i, e in enumerate(offsets):
                if e:
                    start(remote(query, qwin.at[i], q_ss.at[i], q_rs.at[i], blk_peer(n_blk - e)))

    def send_late():
        if line:

            @pl.when(jnp.logical_not(inner))
            def _():
                to_mirror.start()

            started.append(to_mirror)

    def wait_query(t):
        i = position(t)
        remote(query, qwin.at[i], q_ss.at[0], q_rs.at[i], blk_peer(1)).wait_recv()
        if line and t == 1:
            start(handed)

    def offset_at(t):
        return position(t) if line else offsets[t]

    copies1, copies2, copies3, stat_copies = {}, {}, {}, {}

    def part(h):
        return pl.ds(h * half, half)

    def product(t, kk, j, h):
        window = query[...] if t == 0 else qwin[position(t)]
        value = lax.dot_general(
            ordered[kk, j, part(h), :], window, (((1,), (1,)), ((), ())),
            preferred_element_type=F32,
        )
        if kk:
            pown[t, j, part(h), :] = value
        else:
            snd1[t, j, part(h), :] = value.astype(BF16)
            copies1[t, j, h] = start(
                remote(
                    snd1.at[t, j, part(h)], rcv1.at[t, j, part(h)],
                    s1_ss.at[t, j, h], s1_rs.at[t, j, h], sub_peer(0, 0),
                )
            )

    def permute(kk, j, h):
        slot = kk * nx + j
        q = 2 * ((x + j) % nx) + (k if kk else 1 - k)
        wanted = lax.broadcasted_iota(jnp.int32, (half, rows), 0) + (q * share + h * half)
        hot = jnp.where(wanted == ids[...], 1.0, 0.0).astype(BF16)
        value = jnp.dot(hot, train[...], preferred_element_type=F32)
        ordered[kk, j, part(h), :] = value.astype(BF16)
        squares[...] = jnp.broadcast_to(
            jnp.sum(value * value, axis=1, keepdims=True), (half, LANES)
        )
        for b in range(blocks):
            stat_s[slot, h, b : b + 1, :] = to_row(squares[b * lanes : (b + 1) * lanes, :], eye)
        stat_s[slot, h, blocks : blocks + 1, :] = query_row

    def send_stats(h):
        for kk in (0, 1):
            for j in range(nx):
                slot = kk * nx + j
                if slot != nx:
                    stat_copies[slot, h] = start(
                        remote(
                            stat_s.at[slot, h], stat_r.at[slot, h],
                            st_ss.at[slot, h], st_rs.at[slot, h], sub_peer(kk, j),
                        )
                    )

    def stage_a(t, h):
        for j in order:
            for kk in (0, 1):
                product(t, kk, j, h)

    def stage_b(t, h):
        for j in order:
            copies1[t, j, h].wait_recv()
            total = pown[t, j, part(h), :] + rcv1[t, j, part(h), :].astype(F32)
            if j:
                snd2[t, j, part(h), :] = total.astype(BF16)
                copies2[t, j, h] = start(
                    remote(
                        snd2.at[t, j, part(h)], rcv2.at[t, j, part(h)],
                        s2_ss.at[t, j, h], s2_rs.at[t, j, h], sub_peer(1, j),
                    )
                )
            else:
                pown[t, 0, part(h), :] = total

    query_scale = []

    def scales(h):
        stats = stat_s[nx, h]
        for slot in range(n_sub):
            if slot != nx:
                stat_copies[slot, h].wait_recv()
                stats += stat_r[slot, h]
        values = (lax.rsqrt(stats / full + EPS) * full ** (-0.5)).astype(BF16).astype(F32)
        query_scale.append(lax.rsqrt(stats[blocks : blocks + 1, :] / full + EPS))
        for b in range(blocks):
            column = jnp.sum(
                jnp.where(eye, values[b : b + 1, :], 0.0), axis=1, keepdims=True
            )
            scale[pl.ds(h * half + b * lanes, lanes), :] = jnp.broadcast_to(
                column, (lanes, LANES)
            )

    def stage_c(t, h):
        total = pown[t, 0, part(h), :]
        for j in range(1, nx):
            copies2[t, j, h].wait_recv()
            total += rcv2[t, j, part(h), :].astype(F32)
        tile = (total * scale[part(h), :]).astype(BF16)
        if t:
            i = position(t)
            snd3[t, part(h), :] = tile
            copies3[t, h] = start(
                remote(
                    snd3.at[t, part(h)], rcv3.at[i, part(h)],
                    s3_ss.at[t, h], s3_rs.at[i, h], blk_peer(offset_at(t)),
                )
            )
        else:
            write(0, h, tile)

    def write(i, h, tile):
        scored = (tile.astype(F32) * query_scale[0]).astype(BF16)
        for w in range(2 * HOPS + 1):
            if (w - HOPS) % n_blk == offsets[i]:
                out[0, w, part(h), :] = scored

    loads[1].wait()
    loads[2].wait()
    def arrange(h, js):
        for j in js:
            for kk in (0, 1):
                permute(kk, j, h)

    arrange(0, order)
    pl.semaphore_wait(barrier, len(peers))
    send_queries()
    stage_a(0, 0)
    send_stats(0)
    arrange(1, order[: nx // 2])
    stage_b(0, 0)
    arrange(1, order[nx // 2 :])
    send_late()
    stage_a(0, 1)
    send_stats(1)
    stage_b(0, 1)
    wait_query(1)
    stage_a(1, 0)
    stage_b(1, 0)
    stage_a(1, 1)
    stage_b(1, 1)
    scales(0)
    scales(1)
    wait_query(2)
    stage_a(2, 0)
    stage_a(2, 1)
    stage_c(1, 0)
    stage_b(2, 0)
    stage_c(1, 1)
    stage_b(2, 1)
    for t in range(3, nd):
        wait_query(t)
        stage_a(t, 0)
        stage_a(t, 1)
        stage_b(t, 0)
        stage_b(t, 1)
        stage_c(t - 1, 0)
        stage_c(t - 1, 1)
    for t in (0, nd - 1):
        for h in range(PARTS):
            stage_c(t, h)

    for h in range(PARTS):
        for i in range(1, nd):
            remote(
                snd3.at[i, part(h)], rcv3.at[i, part(h)],
                s3_ss.at[i, h], s3_rs.at[i, h], blk_peer(1),
            ).wait_recv()
            write(i, h, rcv3[i, part(h), :])
    for copy in started:
        copy.wait_send()


def local(n_blk, n_sub, train_grads, query_grads, train_ids):
    rows, width = train_grads.shape
    block_rows = query_grads.shape[0]
    share = rows // n_sub
    half = share // PARTS
    nx = n_sub // 2
    nd = len(distinct_offsets(n_blk))
    stat_rows = -(-(half // math.gcd(half, LANES) + 1) // 8) * 8
    win = 2 * HOPS + 1
    dma = pltpu.SemaphoreType.DMA
    hbm = pl.BlockSpec(memory_space=pl.ANY)
    sums = (nd, nx, share, block_rows)
    return pl.pallas_call(
        functools.partial(kernel, n_blk, n_sub),
        out_shape=jax.ShapeDtypeStruct((1, win, share, block_rows), BF16),
        in_specs=[hbm] * 3,
        out_specs=pl.BlockSpec(memory_space=pltpu.VMEM),
        scratch_shapes=[
            pltpu.VMEM((rows, width), BF16),
            pltpu.VMEM((block_rows, width), BF16),
            pltpu.VMEM((1, rows), jnp.int32),
            pltpu.VMEM((2, nx, share, width), BF16),
            pltpu.VMEM((nd, block_rows, width), BF16),
            pltpu.VMEM(sums, F32),
            pltpu.VMEM(sums, BF16),
            pltpu.VMEM(sums, BF16),
            pltpu.VMEM(sums, BF16),
            pltpu.VMEM(sums, BF16),
            pltpu.VMEM((nd, share, block_rows), BF16),
            pltpu.VMEM((nd, share, block_rows), BF16),
            pltpu.VMEM((n_sub, PARTS, stat_rows, LANES), F32),
            pltpu.VMEM((n_sub, PARTS, stat_rows, LANES), F32),
            pltpu.VMEM((half, LANES), F32),
            pltpu.VMEM((share, LANES), F32),
            dma((3,)), dma((max(nd, 4),)), dma((nd,)),
            dma((nd, nx, PARTS)), dma((nd, nx, PARTS)),
            dma((nd, nx, PARTS)), dma((nd, nx, PARTS)),
            dma((nd, PARTS)), dma((nd, PARTS)),
            dma((n_sub, PARTS)), dma((n_sub, PARTS)),
        ],
        compiler_params=pltpu.CompilerParams(
            collective_id=0, has_side_effects=True, vmem_limit_bytes=56 * 1024 * 1024
        ),
    )(train_grads, query_grads, train_ids)


def solution(mesh):
    return jax.shard_map(
        functools.partial(local, mesh.shape["blk"], mesh.shape["sub"]),
        mesh=mesh,
        in_specs=(
            P(("groups", "blk"), "sub"),
            P(("groups", "blk"), "sub"),
            P(("groups", "blk"), None),
        ),
        out_specs=P(("groups", "blk"), None, "sub", None),
        check_vma=False,
    )
```
